32 devices in a mesh: tm: 4 (over y, x), space: 8 (over z, core).
Axes of the slice: x: 2, y: 2, z: 4, core: 2. Of those that a mesh axis runs over, the one named last changes fastest.
Arguments:
- spectrum: float32 [2, 512, 64, 1024], P(None, 'tm', 'space'), may hold values from -6 to 6
- diffusivity: float32 [64, 1024], P('space'), may hold values from 0.5 to 2
Outputs:
- solution: float32 [2, 512, 64, 1024], P(None, 'tm', 'space')
The draws below stay inside these ranges and needn't reach their ends.
All inputs are finite; a program needn't handle non-finite values.
Results may differ from the reference program's by a relative error of at most 0.00016.
Values sent between devices are 32-bit elements; how exact they have to be, the bound alone decides.
A program may use at most 128 MiB of HBM per device.

```python
import math
import jax
import jax.numpy as jnp
import numpy as np
from jax import lax

STEPS = 512
COLS = 1024
ROWS = 64
N_TM = 4


def levels(stream_key, shape, cuts, low, top_value):
    def one(position, shards_of):
        draws = jax.random.uniform(jax.random.fold_in(jax.random.fold_in(stream_key, 6), position), (shards_of,), jnp.float32, low / len(cuts), top_value / len(cuts))
        return jnp.repeat(jnp.exp(draws), shape[position] // shards_of).reshape((-1,) + (1,) * (len(shape) - position - 1))

    gain = one(*cuts[0])
    for cut in cuts[1:]:
        gain = gain * one(*cut)
    return gain


def normal_values(own_key, extent, width, most, split=(), kind=jnp.bfloat16):
    gain = levels(own_key, extent, split, -0.22, 0.18) if split else 1.0
    drawn = jax.random.normal(own_key, extent, jnp.float32) * width * gain
    return jnp.minimum(jnp.maximum(drawn, -most), most).astype(kind)


def setup_inputs(seed: int = 0) -> dict:
    arg_keys = jax.random.split(jax.random.key(seed), 3)
    spectrum = normal_values(arg_keys[0], (2, STEPS, ROWS, COLS), 1.0, 6.0, ((1, 4), (2, 8)), jnp.float32)
    diffusivity = jnp.clip(jnp.exp(math.log(2.0) - 1.3862944 * jax.random.uniform(arg_keys[1], (ROWS, COLS), jnp.float32) ** levels(arg_keys[1], (ROWS, COLS), ((0, 8),), -0.2, 0.2)), 0.5, 2.0)
    return {"spectrum": spectrum, "diffusivity": diffusivity}


alpha_wrap = 0.25
step_rate = 0.5
flow_speed = 2.0
sweep_weights = [1.0 / (1.0 + 0.7 * math.cos(math.pi * (2 * order + 1) / 6.0)) for order in range(3)]

def reverse_bits(number, bit_count):
    result = number * 0
    for bit_place in range(bit_count):
        result = result + (number >> bit_place & 1) * (1 << bit_count - 1 - bit_place)
    return result

def shift_parts(freq_ids, total_steps):
    phase_angle = freq_ids.astype(jnp.float32) * (2.0 * math.pi / total_steps)
    root_scale = alpha_wrap ** (1.0 / total_steps)
    return (step_rate * (1.0 - root_scale * jnp.cos(phase_angle)), step_rate * root_scale * jnp.sin(phase_angle))

def divide_diag(residual, diag_real, diag_imag, magnitude):
    real_part = (residual[0] * diag_real + residual[1] * diag_imag) / magnitude
    imag_part = (residual[1] * diag_real - residual[0] * diag_imag) / magnitude
    return jnp.stack([real_part, imag_part])

def apply_operator(current, diffusion, diag_real, diag_imag):
    padded = jnp.pad(current, ((0, 0), (0, 0), (0, 0), (1, 1)))
    center = padded[:, :, 1:-1, 1:-1]
    from_north = padded[:, :, :-2, 1:-1]
    from_south = padded[:, :, 2:, 1:-1]
    from_west = padded[:, :, 1:-1, :-2]
    from_east = padded[:, :, 1:-1, 2:]
    beside_all = from_north + from_south + from_west + from_east
    real_part = diag_real * center[0] - diag_imag * center[1] - diffusion * beside_all[0] - flow_speed * from_north[0]
    imag_part = diag_real * center[1] + diag_imag * center[0] - diffusion * beside_all[1] - flow_speed * from_north[1]
    return jnp.stack([real_part, imag_part])

def sweeps(right_side, diffusion, lam_real, lam_imag, extend):
    diag_real = lam_real[:, None, None] + 4.0 * diffusion + flow_speed
    diag_imag = lam_imag[:, None, None] + jnp.zeros_like(diag_real)
    magnitude = diag_real * diag_real + diag_imag * diag_imag
    current = sweep_weights[0] * divide_diag(right_side, diag_real, diag_imag, magnitude)
    for order in (1, 2):
        applied = apply_operator(extend(current), diffusion, diag_real, diag_imag)
        current = current + sweep_weights[order] * divide_diag(right_side - applied, diag_real, diag_imag, magnitude)
    return current

def pad_rows(current):
    return jnp.pad(current, ((0, 0), (0, 0), (1, 1), (0, 0)))

def reference(spectrum, diffusivity):
    local_count = STEPS // N_TM
    bit_count = N_TM.bit_length() - 1
    freq_of_pos = np.array([pos % local_count * N_TM + reverse_bits(pos // local_count, bit_count) for pos in range(STEPS)])
    inverse = np.argsort(freq_of_pos)
    natural = spectrum[:, inverse]
    block_size = 16
    blocks = natural.reshape(2, STEPS // block_size, block_size, ROWS, COLS).transpose(1, 0, 2, 3, 4)
    freq_ids = jnp.arange(STEPS, dtype=jnp.int32).reshape(STEPS // block_size, block_size)

    def solve_block(pieces):
        right_side, block_ids = pieces
        lam_real, lam_imag = shift_parts(block_ids, STEPS)
        return sweeps(right_side, diffusivity, lam_real, lam_imag, pad_rows)
    solved = lax.map(solve_block, (blocks, freq_ids))
    solved = solved.transpose(1, 0, 2, 3, 4).reshape(2, STEPS, ROWS, COLS)
    temporal = jnp.fft.ifft(lax.complex(solved[0], solved[1]), axis=0) * math.sqrt(STEPS)
    step_ids = jnp.arange(STEPS, dtype=jnp.int32).astype(jnp.float32)
    factor = jnp.exp(step_ids * (-math.log(alpha_wrap) / STEPS))[:, None, None]
    return jnp.stack([jnp.real(temporal) * factor, jnp.imag(temporal) * factor]).astype(jnp.float32)
```

```python
import functools
import math

import jax
import jax.numpy as jnp
import numpy as np
from jax import lax
from jax.experimental import pallas as pl
from jax.experimental.pallas import tpu as pltpu
from jax.sharding import PartitionSpec as P

alpha_wrap = 0.25
step_rate = 0.5
flow_speed = 2.0
sweep_weights = [
    1.0 / (1.0 + 0.7 * math.cos(math.pi * (2 * order + 1) / 6.0)) for order in range(3)
]
MESH = pl.DeviceIdType.MESH
HALO = 2


def reverse_bits(number, bit_count):
    result = number * 0
    for bit_place in range(bit_count):
        result = result + (number >> bit_place & 1) * (1 << bit_count - 1 - bit_place)
    return result


def make_tables(tm_count, local_count):
    bit_count = tm_count.bit_length() - 1
    total = tm_count * local_count
    place = np.arange(local_count)
    dft = np.zeros((tm_count, 2 * local_count, 2 * local_count))
    shifts = np.zeros((tm_count, 2 * local_count, 128))
    factors = np.zeros((tm_count, bit_count, 4))
    root_scale = alpha_wrap ** (1.0 / total)
    for dev in range(tm_count):
        residue = reverse_bits(dev, bit_count)
        freq = place * tm_count + residue
        phase = 2.0 * np.pi * (place[:, None] * freq[None, :] % total) / total
        grown = alpha_wrap ** (-place / total)[:, None] / math.sqrt(total)
        cosine, sine = grown * np.cos(phase), grown * np.sin(phase)
        dft[dev] = np.block([[cosine, -sine], [sine, cosine]])
        angle = 2.0 * np.pi * freq / total
        shifts[dev, :local_count] = (step_rate * (1.0 - root_scale * np.cos(angle)))[:, None]
        shifts[dev, local_count:] = (step_rate * root_scale * np.sin(angle))[:, None]
        for stage in range(bit_count):
            turn = (dev % (2 << stage)) / (2 << stage)
            unit, spun = (1.0, 0.0), (math.cos(2 * math.pi * turn), math.sin(2 * math.pi * turn))
            mine, theirs = (spun, unit) if dev >> stage & 1 else (unit, spun)
            scale = alpha_wrap ** (-dev / tm_count) if stage == bit_count - 1 else 1.0
            factors[dev, stage] = scale * np.array([*mine, *theirs])
    return (
        dft.astype(np.float32),
        shifts.astype(np.float32),
        factors.reshape(-1).astype(np.float32),
    )


def kernel(
    cfg, field, diffusion, dft_all, shift_all, factors, out,
    hold, mid, last, moved, grid_d, dft, shift,
    load_sem, table_sem, edge_send, edge_recv, move_send, move_recv, out_sem,
):
    stages, tm_count, count, rows, cols, parts, tile = cfg
    width = cols // parts
    d = lax.axis_index("tm")
    s = lax.axis_index("space")
    s_count = lax.axis_size("space")
    is_first, is_last = s == 0, s == s_count - 1
    not_first, not_last = s > 0, s < s_count - 1
    partners = [d + (1 << g) - (2 << g) * ((d // (1 << g)) % 2) for g in range(stages)]

    barrier = pltpu.get_barrier_semaphore()
    for partner in partners:
        pl.semaphore_signal(barrier, inc=1, device_id={"tm": partner}, device_id_type=MESH)

    @pl.when(not_first)
    def _():
        pl.semaphore_signal(barrier, inc=1, device_id={"space": s - 1}, device_id_type=MESH)

    @pl.when(not_last)
    def _():
        pl.semaphore_signal(barrier, inc=1, device_id={"space": s + 1}, device_id_type=MESH)

    row_order = [(turn + HALO) % rows for turn in range(rows)]
    loads = {
        row: pltpu.make_async_copy(field.at[row], hold.at[row + HALO], load_sem.at[row])
        for row in range(rows)
    }
    tables = [
        pltpu.make_async_copy(diffusion, grid_d.at[pl.ds(8, rows)], table_sem.at[0]),
        pltpu.make_async_copy(shift_all.at[d], shift, table_sem.at[1]),
        pltpu.make_async_copy(dft_all.at[d], dft, table_sem.at[2]),
    ]
    tables[0].start()
    tables[1].start()
    for row in range(rows):
        loads[row].start()
    tables[2].start()

    to_north = [
        pltpu.make_async_remote_copy(
            field.at[pl.ds(0, HALO)], hold.at[pl.ds(rows + HALO, HALO)],
            edge_send.at[0], edge_recv.at[0], device_id={"space": s - 1}, device_id_type=MESH),
        pltpu.make_async_remote_copy(
            diffusion, grid_d.at[pl.ds(8 + rows, rows)],
            edge_send.at[1], edge_recv.at[1], device_id={"space": s - 1}, device_id_type=MESH),
    ]
    to_south = [
        pltpu.make_async_remote_copy(
            field.at[pl.ds(rows - HALO, HALO)], hold.at[pl.ds(0, HALO)],
            edge_send.at[2], edge_recv.at[2], device_id={"space": s + 1}, device_id_type=MESH),
        pltpu.make_async_remote_copy(
            diffusion, grid_d.at[pl.ds(8 - rows, rows)],
            edge_send.at[3], edge_recv.at[3], device_id={"space": s + 1}, device_id_type=MESH),
    ]

    beside = lax.div(s + s_count - 1, s_count) + lax.div(2 * (s_count - 1) - s, s_count)
    pl.semaphore_wait(barrier, stages + beside)

    @pl.when(not_first)
    def _():
        for copy in to_north:
            copy.start()

    @pl.when(not_last)
    def _():
        for copy in to_south:
            copy.start()

    tables[0].wait()
    tables[1].wait()

    lanes = lax.broadcasted_iota(jnp.int32, (8, cols), 1)

    def each_block(body):
        def step(index, carry):
            low = pl.multiple_of(index * 8, 8)
            body(pl.ds(low, 8), pl.ds(pl.multiple_of(low + count, 8), 8))
            return carry

        lax.fori_loop(0, count // 8, step, 0)

    def inverse_diag(row, re, im):
        wide = jnp.concatenate
        local = jnp.broadcast_to(grid_d[pl.ds(8 + row, 1), :], (8, cols))
        diag_real = wide([shift[re, :]] * (cols // 128), axis=1) + (4.0 * local + flow_speed)
        diag_imag = wide([shift[im, :]] * (cols // 128), axis=1)
        scale = 1.0 / (diag_real * diag_real + diag_imag * diag_imag)
        return local, diag_real * scale, diag_imag * scale

    def over(real, imag, g_real, g_imag):
        return real * g_real + imag * g_imag, imag * g_real - real * g_imag

    def pull(ref, at, block, local):
        here = ref[at, block, :]
        west = jnp.where(lanes == 0, 0.0, pltpu.roll(here, 1, 1))
        east = jnp.where(lanes == cols - 1, 0.0, pltpu.roll(here, cols - 1, 1))
        north = ref[at - 1, block, :]
        south = ref[at + 1, block, :]
        return here, local * (north + south + west + east) + flow_speed * north

    w0, w1, w2 = sweep_weights

    def first_sweep(row):
        at = row + HALO

        def body(re, im):
            _, g_real, g_imag = inverse_diag(row, re, im)
            real, imag = over(hold[at, re, :], hold[at, im, :], g_real, g_imag)
            hold[at, re, :] = w0 * real
            hold[at, im, :] = w0 * imag

        each_block(body)

    def second_sweep(row):
        at = row + HALO
        keep = 1.0 - w1 + w1 / w0

        def body(re, im):
            local, g_real, g_imag = inverse_diag(row, re, im)
            here_real, pull_real = pull(hold, at, re, local)
            here_imag, pull_imag = pull(hold, at, im, local)
            real, imag = over(pull_real, pull_imag, g_real, g_imag)
            mid[row + 1, re, :] = keep * here_real + w1 * real
            mid[row + 1, im, :] = keep * here_imag + w1 * imag

        each_block(body)

    def third_sweep(row):
        def body(re, im):
            local, g_real, g_imag = inverse_diag(row, re, im)
            here_real, pull_real = pull(mid, row + 1, re, local)
            here_imag, pull_imag = pull(mid, row + 1, im, local)
            real, imag = over(pull_real, pull_imag, g_real, g_imag)
            at = row + HALO
            last[re, :] = (1.0 - w2) * here_real + (w2 / w0) * hold[at, re, :] + w2 * real
            last[im, :] = (1.0 - w2) * here_imag + (w2 / w0) * hold[at, im, :] + w2 * imag

        each_block(body)

    def columns(part):
        return pl.ds(pl.multiple_of(part * width, 128), width)

    def holder(stage, row):
        return hold.at[row + HALO] if stage == 0 else moved.at[stage - 1, row]

    def exchange(stage, row, part):
        cut = columns(part)
        return pltpu.make_async_remote_copy(
            holder(stage, row).at[:, cut], moved.at[stage, row, :, cut],
            move_send.at[stage, row, part], move_recv.at[stage, row, part],
            device_id={"tm": partners[stage]}, device_id_type=MESH)

    def write_out(row, part):
        cut = columns(part)
        return pltpu.make_async_copy(
            moved.at[stages - 1, row, :, cut], out.at[row, :, cut], out_sem.at[row, part])

    def place(chunk):
        return (chunk // parts + HALO) % rows, chunk % parts

    def combine(stage, chunk):
        row, part = place(chunk)
        exchange(stage, row, part).wait()
        cut = columns(part)
        mine, theirs = holder(stage, row), moved.at[stage, row]
        base = (d * stages + stage) * 4
        mr, mi, tr, ti = [factors[base + i] for i in range(4)]

        def body(re, im):
            a_real, a_imag = mine[re, cut], mine[im, cut]
            b_real, b_imag = theirs[re, cut], theirs[im, cut]
            theirs[re, cut] = mr * a_real - mi * a_imag + (tr * b_real - ti * b_imag)
            theirs[im, cut] = mr * a_imag + mi * a_real + (tr * b_imag + ti * b_real)

        each_block(body)
        if stage + 1 < stages:
            exchange(stage + 1, row, part).start()
        else:
            write_out(row, part).start()

    done_first, done_second = set(), set()

    def north_edge():
        @pl.when(not_first)
        def _():
            for copy in to_south:
                copy.wait_recv()
            for row in range(-HALO, 0):
                first_sweep(row)

        @pl.when(is_first)
        def _():
            hold[1] = jnp.zeros((2 * count, cols), jnp.float32)
            mid[0] = jnp.zeros((2 * count, cols), jnp.float32)

        need_first(0)

        @pl.when(not_first)
        def _():
            second_sweep(-1)

    def south_edge():
        @pl.when(not_last)
        def _():
            for copy in to_north:
                copy.wait_recv()
            for row in range(rows, rows + HALO):
                first_sweep(row)

        @pl.when(is_last)
        def _():
            hold[rows + HALO] = jnp.zeros((2 * count, cols), jnp.float32)
            mid[rows + 1] = jnp.zeros((2 * count, cols), jnp.float32)

        need_first(rows - 1)

        @pl.when(not_last)
        def _():
            second_sweep(rows)

    edges = {-1: north_edge, rows: south_edge}

    def need_first(row):
        if row in edges:
            if edges[row] is not None:
                run, edges[row] = edges[row], None
                run()
        elif row not in done_first:
            done_first.add(row)
            loads[row].wait()
            first_sweep(row)

    def need_second(row):
        if row in edges:
            need_first(row)
        elif row not in done_second:
            done_second.add(row)
            for near in (row - 1, row, row + 1):
                need_first(near)
            second_sweep(row)

    def solve_row(row, first):
        for near in (row - 1, row, row + 1):
            need_second(near)
        third_sweep(row)
        if first:
            tables[2].wait()
        for part in range(parts):
            def step(index, carry, part=part):
                cut = pl.ds(pl.multiple_of(part * width + index * tile, 128), tile)
                hold[row + HALO, :, cut] = jnp.dot(
                    dft[...], last[:, cut], precision=lax.Precision.HIGHEST,
                    preferred_element_type=jnp.float32)
                return carry

            lax.fori_loop(0, width // tile, step, 0)
            exchange(0, row, part).start()

    chunks = rows * parts
    lags = [1 + 2 * stage for stage in range(stages)]
    uniform = range(max(rows, lags[-1]), chunks + 1)

    def tick(now, checked):
        for stage in range(stages):
            if not checked or 0 <= now - lags[stage] < chunks:
                combine(stage, now - lags[stage])

    for now in range(uniform.start):
        if now < rows:
            solve_row(row_order[now], now == 0)
        tick(now, True)

    def steady(now, carry):
        tick(now, False)
        return carry

    lax.fori_loop(uniform.start, uniform.stop, steady, 0)
    for now in range(uniform.stop, chunks + lags[-1]):
        tick(now, True)

    def finish(chunk, carry):
        row, part = place(chunk)
        write_out(row, part).wait()
        return carry

    lax.fori_loop(0, chunks, finish, 0)

    @pl.when(not_first)
    def _():
        for copy in to_north:
            copy.wait_send()

    @pl.when(not_last)
    def _():
        for copy in to_south:
            copy.wait_send()


def on_device(spectrum, diffusivity):
    count, rows, cols = spectrum.shape[1:]
    tm_count = lax.axis_size("tm")
    stages = tm_count.bit_length() - 1
    parts, tile = 2, 256
    field = spectrum.transpose(2, 0, 1, 3).reshape(rows, 2 * count, cols)
    dft, shifts, factors = make_tables(tm_count, count)
    cfg = (stages, tm_count, count, rows, cols, parts, tile)
    high = 2 * count
    anywhere = pl.BlockSpec(memory_space=pl.ANY)
    f32 = jnp.float32
    result = pl.pallas_call(
        functools.partial(kernel, cfg),
        out_shape=jax.ShapeDtypeStruct((rows, high, cols), f32),
        in_specs=[anywhere] * 4 + [pl.BlockSpec(memory_space=pltpu.SMEM)],
        out_specs=anywhere,
        scratch_shapes=[
            pltpu.VMEM((rows + 2 * HALO, high, cols), f32),
            pltpu.VMEM((rows + 2, high, cols), f32),
            pltpu.VMEM((high, cols), f32),
            pltpu.VMEM((stages, rows, high, cols), f32),
            pltpu.VMEM((8 + 2 * rows, cols), f32),
            pltpu.VMEM((high, high), f32),
            pltpu.VMEM((high, 128), f32),
            pltpu.SemaphoreType.DMA((rows,)),
            pltpu.SemaphoreType.DMA((3,)),
            pltpu.SemaphoreType.DMA((4,)),
            pltpu.SemaphoreType.DMA((4,)),
            pltpu.SemaphoreType.DMA((stages, rows, parts)),
            pltpu.SemaphoreType.DMA((stages, rows, parts)),
            pltpu.SemaphoreType.DMA((rows, parts)),
        ],
        compiler_params=pltpu.CompilerParams(
            collective_id=0, has_side_effects=True, vmem_limit_bytes=50 * 2**20),
        cost_estimate=pl.CostEstimate(
            flops=12 * high * high * rows * cols, bytes_accessed=8 * rows * high * cols,
            transcendentals=0),
    )(field, diffusivity, jnp.asarray(dft), jnp.asarray(shifts), jnp.asarray(factors))
    return result.reshape(rows, 2, count, cols).transpose(1, 2, 0, 3)


def solution(mesh):
    in_specs = (P(None, "tm", "space", None), P("space", None))
    out_specs = P(None, "tm", "space", None)
    return jax.shard_map(
        on_device, mesh=mesh, in_specs=in_specs, out_specs=out_specs, check_vma=False
    )
```

```python
import functools
import math

import jax
import jax.numpy as jnp
import numpy as np
from jax import lax
from jax.experimental import pallas as pl
from jax.experimental.pallas import tpu as pltpu
from jax.sharding import PartitionSpec as P

alpha_wrap = 0.25
step_rate = 0.5
flow_speed = 2.0
sweep_weights = [
    1.0 / (1.0 + 0.7 * math.cos(math.pi * (2 * order + 1) / 6.0)) for order in range(3)
]
MESH = pl.DeviceIdType.MESH
HALO = 2
GROUPS = 4


def reverse_bits(number, bit_count):
    result = number * 0
    for bit_place in range(bit_count):
        result = result + (number >> bit_place & 1) * (1 << bit_count - 1 - bit_place)
    return result


def make_tables(tm_count, local_count):
    bit_count = tm_count.bit_length() - 1
    total = tm_count * local_count
    place = np.arange(local_count)
    dft = np.zeros((tm_count, 2 * local_count, 2 * local_count))
    shifts = np.zeros((tm_count, 2 * local_count, 128))
    factors = np.zeros((tm_count, bit_count, 4))
    root_scale = alpha_wrap ** (1.0 / total)
    for dev in range(tm_count):
        residue = reverse_bits(dev, bit_count)
        freq = place * tm_count + residue
        phase = 2.0 * np.pi * (place[:, None] * freq[None, :] % total) / total
        grown = alpha_wrap ** (-place / total)[:, None] / math.sqrt(total)
        cosine, sine = grown * np.cos(phase), grown * np.sin(phase)
        dft[dev] = np.block([[cosine, -sine], [sine, cosine]])
        angle = 2.0 * np.pi * freq / total
        shifts[dev, :local_count] = (step_rate * (1.0 - root_scale * np.cos(angle)))[:, None]
        shifts[dev, local_count:] = (step_rate * root_scale * np.sin(angle))[:, None]
        for stage in range(bit_count):
            turn = (dev % (2 << stage)) / (2 << stage)
            unit, spun = (1.0, 0.0), (math.cos(2 * math.pi * turn), math.sin(2 * math.pi * turn))
            mine, theirs = (spun, unit) if dev >> stage & 1 else (unit, spun)
            scale = alpha_wrap ** (-dev / tm_count) if stage == bit_count - 1 else 1.0
            factors[dev, stage] = scale * np.array([*mine, *theirs])
    return (
        dft.astype(np.float32),
        shifts.astype(np.float32),
        factors.reshape(-1).astype(np.float32),
    )


def kernel(
    cfg, field, diffusion, dft_all, shift_all, factors, out,
    raw, hold, mid, last, moved, grid_d, dft, shift,
    load_sem, table_sem, edge_send, edge_recv, move_send, move_recv, out_sem,
):
    stages, tm_count, count, rows, cols, parts, tile = cfg
    width = cols // parts
    d = lax.axis_index("tm")
    s = lax.axis_index("space")
    s_count = lax.axis_size("space")
    is_first, is_last = s == 0, s == s_count - 1
    not_first, not_last = s > 0, s < s_count - 1
    partners = [d + (1 << g) - (2 << g) * ((d // (1 << g)) % 2) for g in range(stages)]

    barrier = pltpu.get_barrier_semaphore()
    for partner in partners:
        pl.semaphore_signal(barrier, inc=1, device_id={"tm": partner}, device_id_type=MESH)

    @pl.when(not_first)
    def _():
        pl.semaphore_signal(barrier, inc=1, device_id={"space": s - 1}, device_id_type=MESH)

    @pl.when(not_last)
    def _():
        pl.semaphore_signal(barrier, inc=1, device_id={"space": s + 1}, device_id_type=MESH)

    row_order = [(turn + HALO) % rows for turn in range(rows)]
    group = count // GROUPS
    loads = [
        [
            pltpu.make_async_copy(
                field.at[pl.ds(half * count + part * group, group)],
                raw.at[pl.ds(half * count + part * group, group)], load_sem.at[part, half])
            for half in range(2)
        ]
        for part in range(GROUPS)
    ]
    tables = [
        pltpu.make_async_copy(diffusion, grid_d.at[pl.ds(8, rows)], table_sem.at[0]),
        pltpu.make_async_copy(shift_all.at[d], shift, table_sem.at[1]),
        pltpu.make_async_copy(dft_all.at[d], dft, table_sem.at[2]),
    ]
    tables[0].start()
    tables[1].start()
    for pair in loads:
        for copy in pair:
            copy.start()
    tables[2].start()

    to_north = [
        pltpu.make_async_remote_copy(
            hold.at[pl.ds(HALO, HALO)], hold.at[pl.ds(rows + HALO, HALO)],
            edge_send.at[0], edge_recv.at[0], device_id={"space": s - 1}, device_id_type=MESH),
        pltpu.make_async_remote_copy(
            diffusion, grid_d.at[pl.ds(8 + rows, rows)],
            edge_send.at[1], edge_recv.at[1], device_id={"space": s - 1}, device_id_type=MESH),
    ]
    to_south = [
        pltpu.make_async_remote_copy(
            hold.at[pl.ds(rows, HALO)], hold.at[pl.ds(0, HALO)],
            edge_send.at[2], edge_recv.at[2], device_id={"space": s + 1}, device_id_type=MESH),
        pltpu.make_async_remote_copy(
            diffusion, grid_d.at[pl.ds(8 - rows, rows)],
            edge_send.at[3], edge_recv.at[3], device_id={"space": s + 1}, device_id_type=MESH),
    ]

    tables[0].wait()
    tables[1].wait()

    lanes = lax.broadcasted_iota(jnp.int32, (8, cols), 1)

    def each_block(body):
        def step(index, carry):
            low = pl.multiple_of(index * 8, 8)
            body(pl.ds(low, 8), pl.ds(pl.multiple_of(low + count, 8), 8))
            return carry

        lax.fori_loop(0, count // 8, step, 0)

    def inverse_diag(row, re, im, cut=slice(None), span=None):
        span = span or cols
        wide = jnp.concatenate
        local = jnp.broadcast_to(grid_d[pl.ds(8 + row, 1), cut], (8, span))
        diag_real = wide([shift[re, :]] * (span // 128), axis=1) + (4.0 * local + flow_speed)
        diag_imag = wide([shift[im, :]] * (span // 128), axis=1)
        scale = 1.0 / (diag_real * diag_real + diag_imag * diag_imag)
        return local, diag_real * scale, diag_imag * scale

    def over(real, imag, g_real, g_imag):
        return real * g_real + imag * g_imag, imag * g_real - real * g_imag

    def pull(ref, at, block, local):
        here = ref[at, block, :]
        west = jnp.where(lanes == 0, 0.0, pltpu.roll(here, 1, 1))
        east = jnp.where(lanes == cols - 1, 0.0, pltpu.roll(here, cols - 1, 1))
        north = ref[at - 1, block, :]
        south = ref[at + 1, block, :]
        return here, local * (north + south + west + east) + flow_speed * north

    w0, w1, w2 = sweep_weights

    def first_sweep(part):
        def step(index, carry):
            low = part * group + index // (cols // tile) * 8
            cut = pl.ds(pl.multiple_of(index % (cols // tile) * tile, 128), tile)
            re = pl.ds(pl.multiple_of(low, 8), 8)
            im = pl.ds(pl.multiple_of(low + count, 8), 8)
            real_rows = jnp.swapaxes(raw[re, :, cut], 0, 1)
            imag_rows = jnp.swapaxes(raw[im, :, cut], 0, 1)
            for row in range(rows):
                _, g_real, g_imag = inverse_diag(row, re, im, cut, tile)
                real, imag = over(real_rows[row], imag_rows[row], g_real, g_imag)
                hold[row + HALO, re, cut] = w0 * real
                hold[row + HALO, im, cut] = w0 * imag
            return carry

        lax.fori_loop(0, group // 8 * (cols // tile), step, 0)

    def second_sweep(row):
        at = row + HALO
        keep = 1.0 - w1 + w1 / w0

        def body(re, im):
            local, g_real, g_imag = inverse_diag(row, re, im)
            here_real, pull_real = pull(hold, at, re, local)
            here_imag, pull_imag = pull(hold, at, im, local)
            real, imag = over(pull_real, pull_imag, g_real, g_imag)
            mid[row + 1, re, :] = keep * here_real + w1 * real
            mid[row + 1, im, :] = keep * here_imag + w1 * imag

        each_block(body)

    def third_sweep(row):
        def body(re, im):
            local, g_real, g_imag = inverse_diag(row, re, im)
            here_real, pull_real = pull(mid, row + 1, re, local)
            here_imag, pull_imag = pull(mid, row + 1, im, local)
            real, imag = over(pull_real, pull_imag, g_real, g_imag)
            at = row + HALO
            last[re, :] = (1.0 - w2) * here_real + (w2 / w0) * hold[at, re, :] + w2 * real
            last[im, :] = (1.0 - w2) * here_imag + (w2 / w0) * hold[at, im, :] + w2 * imag

        each_block(body)

    def columns(part):
        return pl.ds(pl.multiple_of(part * width, 128), width)

    def holder(stage, row):
        return hold.at[row + HALO] if stage == 0 else moved.at[stage - 1, row]

    def exchange(stage, row, part):
        cut = columns(part)
        return pltpu.make_async_remote_copy(
            holder(stage, row).at[:, cut], moved.at[stage, row, :, cut],
            move_send.at[stage, row, part], move_recv.at[stage, row, part],
            device_id={"tm": partners[stage]}, device_id_type=MESH)

    def write_out(row, part):
        cut = columns(part)
        return pltpu.make_async_copy(
            moved.at[stages - 1, row, :, cut], out.at[row, :, cut], out_sem.at[row, part])

    def place(chunk):
        return (chunk // parts + HALO) % rows, chunk % parts

    def combine(stage, chunk):
        row, part = place(chunk)
        exchange(stage, row, part).wait()
        cut = columns(part)
        mine, theirs = holder(stage, row), moved.at[stage, row]
        base = (d * stages + stage) * 4
        mr, mi, tr, ti = [factors[base + i] for i in range(4)]

        def body(re, im):
            a_real, a_imag = mine[re, cut], mine[im, cut]
            b_real, b_imag = theirs[re, cut], theirs[im, cut]
            theirs[re, cut] = mr * a_real - mi * a_imag + (tr * b_real - ti * b_imag)
            theirs[im, cut] = mr * a_imag + mi * a_real + (tr * b_imag + ti * b_real)

        each_block(body)
        if stage + 1 < stages:
            exchange(stage + 1, row, part).start()
        else:
            write_out(row, part).start()

    for part in range(GROUPS):
        for copy in loads[part]:
            copy.wait()
        first_sweep(part)

    beside = lax.div(s + s_count - 1, s_count) + lax.div(2 * (s_count - 1) - s, s_count)
    pl.semaphore_wait(barrier, stages + beside)

    @pl.when(not_first)
    def _():
        for copy in to_north:
            copy.start()

    @pl.when(not_last)
    def _():
        for copy in to_south:
            copy.start()

    done = set()

    def north_edge():
        @pl.when(not_first)
        def _():
            for copy in to_south:
                copy.wait_recv()
            second_sweep(-1)

        @pl.when(is_first)
        def _():
            hold[HALO - 1] = jnp.zeros((2 * count, cols), jnp.float32)
            mid[0] = jnp.zeros((2 * count, cols), jnp.float32)

    def south_edge():
        @pl.when(not_last)
        def _():
            for copy in to_north:
                copy.wait_recv()
            second_sweep(rows)

        @pl.when(is_last)
        def _():
            hold[rows + HALO] = jnp.zeros((2 * count, cols), jnp.float32)
            mid[rows + 1] = jnp.zeros((2 * count, cols), jnp.float32)

    def need_second(row):
        if row in done:
            return
        done.add(row)
        if row == -1:
            north_edge()
        elif row == rows:
            south_edge()
        else:
            if row == 0:
                need_second(-1)
            if row == rows - 1:
                need_second(rows)
            second_sweep(row)

    def solve_row(row, first):
        for near in (row - 1, row, row + 1):
            need_second(near)
        third_sweep(row)
        if row == 0:
            @pl.when(not_first)
            def _():
                to_north[0].wait_send()

        if row == rows - HALO:
            @pl.when(not_last)
            def _():
                to_south[0].wait_send()

        if first:
            tables[2].wait()
        for part in range(parts):
            def step(index, carry, part=part):
                cut = pl.ds(pl.multiple_of(part * width + index * tile, 128), tile)
                hold[row + HALO, :, cut] = jnp.dot(
                    dft[...], last[:, cut], precision=lax.Precision.HIGHEST,
                    preferred_element_type=jnp.float32)
                return carry

            lax.fori_loop(0, width // tile, step, 0)
            exchange(0, row, part).start()

    chunks = rows * parts
    lags = [1 + 2 * stage for stage in range(stages)]
    uniform = range(max(rows, lags[-1]), chunks + 1)

    def tick(now, checked):
        for stage in range(stages):
            if not checked or 0 <= now - lags[stage] < chunks:
                combine(stage, now - lags[stage])

    for now in range(uniform.start):
        if now < rows:
            solve_row(row_order[now], now == 0)
        tick(now, True)

    def steady(now, carry):
        tick(now, False)
        return carry

    lax.fori_loop(uniform.start, uniform.stop, steady, 0)
    for now in range(uniform.stop, chunks + lags[-1]):
        tick(now, True)

    def finish(chunk, carry):
        row, part = place(chunk)
        write_out(row, part).wait()
        return carry

    lax.fori_loop(0, chunks, finish, 0)

    @pl.when(not_first)
    def _():
        to_north[1].wait_send()

    @pl.when(not_last)
    def _():
        to_south[1].wait_send()


def swap_kernel(source, target):
    target[...] = jnp.swapaxes(source[...], 0, 1)


def swap_rows(field):
    rows, high, cols = field.shape
    block = 32
    return pl.pallas_call(
        swap_kernel,
        grid=(high // block,),
        out_shape=jax.ShapeDtypeStruct((high, rows, cols), field.dtype),
        in_specs=[pl.BlockSpec((rows, block, cols), lambda i: (0, i, 0))],
        out_specs=pl.BlockSpec((block, rows, cols), lambda i: (i, 0, 0)),
        compiler_params=pltpu.CompilerParams(vmem_limit_bytes=60 * 2**20),
    )(field)


def on_device(spectrum, diffusivity):
    count, rows, cols = spectrum.shape[1:]
    tm_count = lax.axis_size("tm")
    stages = tm_count.bit_length() - 1
    parts, tile = 4, 256
    field = spectrum.reshape(2 * count, rows, cols)
    dft, shifts, factors = make_tables(tm_count, count)
    cfg = (stages, tm_count, count, rows, cols, parts, tile)
    high = 2 * count
    anywhere = pl.BlockSpec(memory_space=pl.ANY)
    f32 = jnp.float32
    result = pl.pallas_call(
        functools.partial(kernel, cfg),
        out_shape=jax.ShapeDtypeStruct((rows, high, cols), f32),
        in_specs=[anywhere] * 4 + [pl.BlockSpec(memory_space=pltpu.SMEM)],
        out_specs=anywhere,
        scratch_shapes=[
            pltpu.VMEM((high, rows, cols), f32),
            pltpu.VMEM((rows + 2 * HALO, high, cols), f32),
            pltpu.VMEM((rows + 2, high, cols), f32),
            pltpu.VMEM((high, cols), f32),
            pltpu.VMEM((stages, rows, high, cols), f32),
            pltpu.VMEM((8 + 2 * rows, cols), f32),
            pltpu.VMEM((high, high), f32),
            pltpu.VMEM((high, 128), f32),
            pltpu.SemaphoreType.DMA((GROUPS, 2)),
            pltpu.SemaphoreType.DMA((3,)),
            pltpu.SemaphoreType.DMA((4,)),
            pltpu.SemaphoreType.DMA((4,)),
            pltpu.SemaphoreType.DMA((stages, rows, parts)),
            pltpu.SemaphoreType.DMA((stages, rows, parts)),
            pltpu.SemaphoreType.DMA((rows, parts)),
        ],
        compiler_params=pltpu.CompilerParams(
            collective_id=0, has_side_effects=True, vmem_limit_bytes=56 * 2**20),
        cost_estimate=pl.CostEstimate(
            flops=12 * high * high * rows * cols, bytes_accessed=8 * rows * high * cols,
            transcendentals=0),
    )(field, diffusivity, jnp.asarray(dft), jnp.asarray(shifts), jnp.asarray(factors))
    return swap_rows(result).reshape(2, count, rows, cols)


def solution(mesh):
    in_specs = (P(None, "tm", "space", None), P("space", None))
    out_specs = P(None, "tm", "space", None)
    return jax.shard_map(
        on_device, mesh=mesh, in_specs=in_specs, out_specs=out_specs, check_vma=False
    )
```

```python
import functools
import math

import jax
import jax.numpy as jnp
import numpy as np
from jax import lax
from jax.experimental import pallas as pl
from jax.experimental.pallas import tpu as pltpu
from jax.sharding import PartitionSpec as P

alpha_wrap = 0.25
step_rate = 0.5
flow_speed = 2.0
sweep_weights = [
    1.0 / (1.0 + 0.7 * math.cos(math.pi * (2 * order + 1) / 6.0)) for order in range(3)
]
MESH = pl.DeviceIdType.MESH
HALO = 2
GROUPS = 4


def reverse_bits(number, bit_count):
    result = number * 0
    for bit_place in range(bit_count):
        result = result + (number >> bit_place & 1) * (1 << bit_count - 1 - bit_place)
    return result


def make_tables(tm_count, local_count):
    bit_count = tm_count.bit_length() - 1
    total = tm_count * local_count
    place = np.arange(local_count)
    dft = np.zeros((tm_count, 2 * local_count, 2 * local_count))
    shifts = np.zeros((tm_count, 2 * local_count, 128))
    factors = np.zeros((tm_count, bit_count, 4))
    root_scale = alpha_wrap ** (1.0 / total)
    for dev in range(tm_count):
        residue = reverse_bits(dev, bit_count)
        freq = place * tm_count + residue
        phase = 2.0 * np.pi * (place[:, None] * freq[None, :] % total) / total
        grown = alpha_wrap ** (-place / total)[:, None] / math.sqrt(total)
        cosine, sine = grown * np.cos(phase), grown * np.sin(phase)
        dft[dev] = np.block([[cosine, -sine], [sine, cosine]])
        angle = 2.0 * np.pi * freq / total
        shifts[dev, :local_count] = (step_rate * (1.0 - root_scale * np.cos(angle)))[:, None]
        shifts[dev, local_count:] = (step_rate * root_scale * np.sin(angle))[:, None]
        for stage in range(bit_count):
            turn = (dev % (2 << stage)) / (2 << stage)
            unit, spun = (1.0, 0.0), (math.cos(2 * math.pi * turn), math.sin(2 * math.pi * turn))
            mine, theirs = (spun, unit) if dev >> stage & 1 else (unit, spun)
            scale = alpha_wrap ** (-dev / tm_count) if stage == bit_count - 1 else 1.0
            factors[dev, stage] = scale * np.array([*mine, *theirs])
    return (
        dft.astype(np.float32),
        shifts.astype(np.float32),
        factors.reshape(-1).astype(np.float32),
    )


def kernel(
    cfg, field, diffusion, dft_all, shift_all, factors, out,
    raw, hold, mid, last, moved, grid_d, dft, shift,
    load_sem, table_sem, edge_send, edge_recv, move_send, move_recv, out_sem,
):
    stages, tm_count, count, rows, cols, parts, tile = cfg
    width = cols // parts
    d = lax.axis_index("tm")
    s = lax.axis_index("space")
    s_count = lax.axis_size("space")
    is_first, is_last = s == 0, s == s_count - 1
    not_first, not_last = s > 0, s < s_count - 1
    partners = [d + (1 << g) - (2 << g) * ((d // (1 << g)) % 2) for g in range(stages)]

    barrier = pltpu.get_barrier_semaphore()
    for partner in partners:
        pl.semaphore_signal(barrier, inc=1, device_id={"tm": partner}, device_id_type=MESH)

    @pl.when(not_first)
    def _():
        pl.semaphore_signal(barrier, inc=1, device_id={"space": s - 1}, device_id_type=MESH)

    @pl.when(not_last)
    def _():
        pl.semaphore_signal(barrier, inc=1, device_id={"space": s + 1}, device_id_type=MESH)

    row_order = [(turn + HALO) % rows for turn in range(rows)]
    group = count // GROUPS
    loads = [
        [
            pltpu.make_async_copy(
                field.at[pl.ds(half * count + part * group, group)],
                raw.at[pl.ds(half * count + part * group, group)], load_sem.at[part, half])
            for half in range(2)
        ]
        for part in range(GROUPS)
    ]
    tables = [
        pltpu.make_async_copy(diffusion, grid_d.at[pl.ds(8, rows)], table_sem.at[0]),
        pltpu.make_async_copy(shift_all.at[d], shift, table_sem.at[1]),
        pltpu.make_async_copy(dft_all.at[d], dft, table_sem.at[2]),
    ]
    tables[0].start()
    tables[1].start()
    for pair in loads:
        for copy in pair:
            copy.start()
    tables[2].start()

    to_north = [
        pltpu.make_async_remote_copy(
            hold.at[pl.ds(HALO, HALO)], hold.at[pl.ds(rows + HALO, HALO)],
            edge_send.at[0], edge_recv.at[0], device_id={"space": s - 1}, device_id_type=MESH),
        pltpu.make_async_remote_copy(
            diffusion, grid_d.at[pl.ds(8 + rows, rows)],
            edge_send.at[1], edge_recv.at[1], device_id={"space": s - 1}, device_id_type=MESH),
    ]
    to_south = [
        pltpu.make_async_remote_copy(
            hold.at[pl.ds(rows, HALO)], hold.at[pl.ds(0, HALO)],
            edge_send.at[2], edge_recv.at[2], device_id={"space": s + 1}, device_id_type=MESH),
        pltpu.make_async_remote_copy(
            diffusion, grid_d.at[pl.ds(8 - rows, rows)],
            edge_send.at[3], edge_recv.at[3], device_id={"space": s + 1}, device_id_type=MESH),
    ]

    tables[0].wait()
    tables[1].wait()

    lanes = lax.broadcasted_iota(jnp.int32, (8, cols), 1)

    def each_block(body):
        def step(index, carry):
            low = pl.multiple_of(index * 8, 8)
            body(pl.ds(low, 8), pl.ds(pl.multiple_of(low + count, 8), 8))
            return carry

        lax.fori_loop(0, count // 8, step, 0)

    def inverse_diag(row, re, im, cut=slice(None), span=None):
        span = span or cols
        wide = jnp.concatenate
        local = jnp.broadcast_to(grid_d[pl.ds(8 + row, 1), cut], (8, span))
        diag_real = wide([shift[re, :]] * (span // 128), axis=1) + (4.0 * local + flow_speed)
        diag_imag = wide([shift[im, :]] * (span // 128), axis=1)
        magnitude = diag_real * diag_real + diag_imag * diag_imag
        guess = pl.reciprocal(magnitude, approx=True)
        guess = guess * (2.0 - magnitude * guess)
        scale = guess * (2.0 - magnitude * guess)
        return local, diag_real * scale, diag_imag * scale

    def kept_inverse(row, re, im):
        if not 0 <= row < rows:
            return inverse_diag(row, re, im)
        local = jnp.broadcast_to(grid_d[pl.ds(8 + row, 1), :], (8, cols))
        return local, raw[re.start + row], raw[im.start + row]

    def over(real, imag, g_real, g_imag):
        return real * g_real + imag * g_imag, imag * g_real - real * g_imag

    def pull(ref, at, block, local):
        here = ref[at, block, :]
        west = jnp.where(lanes == 0, 0.0, pltpu.roll(here, 1, 1))
        east = jnp.where(lanes == cols - 1, 0.0, pltpu.roll(here, cols - 1, 1))
        north = ref[at - 1, block, :]
        south = ref[at + 1, block, :]
        return here, local * (north + south + west + east) + flow_speed * north

    w0, w1, w2 = sweep_weights

    def first_sweep(part):
        def step(index, carry):
            low = part * group + index // (cols // tile) * 8
            cut = pl.ds(pl.multiple_of(index % (cols // tile) * tile, 128), tile)
            re = pl.ds(pl.multiple_of(low, 8), 8)
            im = pl.ds(pl.multiple_of(low + count, 8), 8)
            real_rows = jnp.swapaxes(raw[re, :, cut], 0, 1)
            imag_rows = jnp.swapaxes(raw[im, :, cut], 0, 1)
            for row in range(rows):
                _, g_real, g_imag = inverse_diag(row, re, im, cut, tile)
                real, imag = over(real_rows[row], imag_rows[row], g_real, g_imag)
                hold[row + HALO, re, cut] = w0 * real
                hold[row + HALO, im, cut] = w0 * imag
                raw[low + row, :, cut] = g_real
                raw[low + count + row, :, cut] = g_imag
            return carry

        lax.fori_loop(0, group // 8 * (cols // tile), step, 0)

    def second_sweep(row):
        at = row + HALO
        keep = 1.0 - w1 + w1 / w0

        def body(re, im):
            local, g_real, g_imag = kept_inverse(row, re, im)
            here_real, pull_real = pull(hold, at, re, local)
            here_imag, pull_imag = pull(hold, at, im, local)
            real, imag = over(pull_real, pull_imag, g_real, g_imag)
            mid[row + 1, re, :] = keep * here_real + w1 * real
            mid[row + 1, im, :] = keep * here_imag + w1 * imag

        each_block(body)

    def third_sweep(row):
        def body(re, im):
            local, g_real, g_imag = kept_inverse(row, re, im)
            here_real, pull_real = pull(mid, row + 1, re, local)
            here_imag, pull_imag = pull(mid, row + 1, im, local)
            real, imag = over(pull_real, pull_imag, g_real, g_imag)
            at = row + HALO
            last[re, :] = (1.0 - w2) * here_real + (w2 / w0) * hold[at, re, :] + w2 * real
            last[im, :] = (1.0 - w2) * here_imag + (w2 / w0) * hold[at, im, :] + w2 * imag

        each_block(body)

    def columns(part):
        return pl.ds(pl.multiple_of(part * width, 128), width)

    def holder(stage, row):
        return hold.at[row + HALO] if stage == 0 else moved.at[stage - 1, row]

    def exchange(stage, row, part):
        cut = columns(part)
        return pltpu.make_async_remote_copy(
            holder(stage, row).at[:, cut], moved.at[stage, row, :, cut],
            move_send.at[stage, row, part], move_recv.at[stage, row, part],
            device_id={"tm": partners[stage]}, device_id_type=MESH)

    def write_out(row, part):
        cut = columns(part)
        return pltpu.make_async_copy(
            moved.at[stages - 1, row, :, cut], out.at[row, :, cut], out_sem.at[row, part])

    def place(chunk):
        return (chunk // parts + HALO) % rows, chunk % parts

    def combine(stage, chunk):
        row, part = place(chunk)
        exchange(stage, row, part).wait()
        cut = columns(part)
        mine, theirs = holder(stage, row), moved.at[stage, row]
        base = (d * stages + stage) * 4
        mr, mi, tr, ti = [factors[base + i] for i in range(4)]

        def body(re, im):
            a_real, a_imag = mine[re, cut], mine[im, cut]
            b_real, b_imag = theirs[re, cut], theirs[im, cut]
            theirs[re, cut] = mr * a_real - mi * a_imag + (tr * b_real - ti * b_imag)
            theirs[im, cut] = mr * a_imag + mi * a_real + (tr * b_imag + ti * b_real)

        each_block(body)
        if stage + 1 < stages:
            exchange(stage + 1, row, part).start()
        else:
            write_out(row, part).start()

    for part in range(GROUPS):
        for copy in loads[part]:
            copy.wait()
        first_sweep(part)

    beside = lax.div(s + s_count - 1, s_count) + lax.div(2 * (s_count - 1) - s, s_count)
    pl.semaphore_wait(barrier, stages + beside)

    @pl.when(not_first)
    def _():
        for copy in to_north:
            copy.start()

    @pl.when(not_last)
    def _():
        for copy in to_south:
            copy.start()

    done = set()

    def north_edge():
        @pl.when(not_first)
        def _():
            for copy in to_south:
                copy.wait_recv()
            second_sweep(-1)

        @pl.when(is_first)
        def _():
            hold[HALO - 1] = jnp.zeros((2 * count, cols), jnp.float32)
            mid[0] = jnp.zeros((2 * count, cols), jnp.float32)

    def south_edge():
        @pl.when(not_last)
        def _():
            for copy in to_north:
                copy.wait_recv()
            second_sweep(rows)

        @pl.when(is_last)
        def _():
            hold[rows + HALO] = jnp.zeros((2 * count, cols), jnp.float32)
            mid[rows + 1] = jnp.zeros((2 * count, cols), jnp.float32)

    def need_second(row):
        if row in done:
            return
        done.add(row)
        if row == -1:
            north_edge()
        elif row == rows:
            south_edge()
        else:
            if row == 0:
                need_second(-1)
            if row == rows - 1:
                need_second(rows)
            second_sweep(row)

    def solve_row(row, first):
        for near in (row - 1, row, row + 1):
            need_second(near)
        third_sweep(row)
        if row == 0:
            @pl.when(not_first)
            def _():
                to_north[0].wait_send()

        if row == rows - HALO:
            @pl.when(not_last)
            def _():
                to_south[0].wait_send()

        if first:
            tables[2].wait()
        for part in range(parts):
            def step(index, carry, part=part):
                cut = pl.ds(pl.multiple_of(part * width + index * tile, 128), tile)
                hold[row + HALO, :, cut] = jnp.dot(
                    dft[...], last[:, cut], precision=lax.Precision.HIGHEST,
                    preferred_element_type=jnp.float32)
                return carry

            lax.fori_loop(0, width // tile, step, 0)
            exchange(0, row, part).start()

    chunks = rows * parts
    lags = [2 * stage for stage in range(stages)]
    pace = 2

    def tick(now, checked):
        for stage in range(stages):
            if not checked or 0 <= now - lags[stage] < chunks:
                combine(stage, now - lags[stage])

    solve_row(row_order[0], True)
    for turn in range(1, rows):
        solve_row(row_order[turn], False)
        for now in range(pace * (turn - 1), pace * turn):
            tick(now, True)
    begin = pace * (rows - 1)

    def steady(now, carry):
        tick(now, False)
        return carry

    lax.fori_loop(begin, chunks, steady, 0)
    for now in range(chunks, chunks + lags[-1]):
        tick(now, True)

    def finish(chunk, carry):
        row, part = place(chunk)
        write_out(row, part).wait()
        return carry

    lax.fori_loop(0, chunks, finish, 0)

    @pl.when(not_first)
    def _():
        to_north[1].wait_send()

    @pl.when(not_last)
    def _():
        to_south[1].wait_send()


def swap_kernel(source, target):
    target[...] = jnp.swapaxes(source[...], 0, 1)


def swap_rows(field):
    rows, high, cols = field.shape
    block = 32
    return pl.pallas_call(
        swap_kernel,
        grid=(high // block,),
        out_shape=jax.ShapeDtypeStruct((high, rows, cols), field.dtype),
        in_specs=[pl.BlockSpec((rows, block, cols), lambda i: (0, i, 0))],
        out_specs=pl.BlockSpec((block, rows, cols), lambda i: (i, 0, 0)),
        compiler_params=pltpu.CompilerParams(vmem_limit_bytes=60 * 2**20),
    )(field)


def on_device(spectrum, diffusivity):
    count, rows, cols = spectrum.shape[1:]
    tm_count = lax.axis_size("tm")
    stages = tm_count.bit_length() - 1
    parts, tile = 4, 256
    field = spectrum.reshape(2 * count, rows, cols)
    dft, shifts, factors = make_tables(tm_count, count)
    cfg = (stages, tm_count, count, rows, cols, parts, tile)
    high = 2 * count
    anywhere = pl.BlockSpec(memory_space=pl.ANY)
    f32 = jnp.float32
    result = pl.pallas_call(
        functools.partial(kernel, cfg),
        out_shape=jax.ShapeDtypeStruct((rows, high, cols), f32),
        in_specs=[anywhere] * 4 + [pl.BlockSpec(memory_space=pltpu.SMEM)],
        out_specs=anywhere,
        scratch_shapes=[
            pltpu.VMEM((high, rows, cols), f32),
            pltpu.VMEM((rows + 2 * HALO, high, cols), f32),
            pltpu.VMEM((rows + 2, high, cols), f32),
            pltpu.VMEM((high, cols), f32),
            pltpu.VMEM((stages, rows, high, cols), f32),
            pltpu.VMEM((8 + 2 * rows, cols), f32),
            pltpu.VMEM((high, high), f32),
            pltpu.VMEM((high, 128), f32),
            pltpu.SemaphoreType.DMA((GROUPS, 2)),
            pltpu.SemaphoreType.DMA((3,)),
            pltpu.SemaphoreType.DMA((4,)),
            pltpu.SemaphoreType.DMA((4,)),
            pltpu.SemaphoreType.DMA((stages, rows, parts)),
            pltpu.SemaphoreType.DMA((stages, rows, parts)),
            pltpu.SemaphoreType.DMA((rows, parts)),
        ],
        compiler_params=pltpu.CompilerParams(
            collective_id=0, has_side_effects=True, vmem_limit_bytes=56 * 2**20),
        cost_estimate=pl.CostEstimate(
            flops=12 * high * high * rows * cols, bytes_accessed=8 * rows * high * cols,
            transcendentals=0),
    )(field, diffusivity, jnp.asarray(dft), jnp.asarray(shifts), jnp.asarray(factors))
    return swap_rows(result).reshape(2, count, rows, cols)


def solution(mesh):
    in_specs = (P(None, "tm", "space", None), P("space", None))
    out_specs = P(None, "tm", "space", None)
    return jax.shard_map(
        on_device, mesh=mesh, in_specs=in_specs, out_specs=out_specs, check_vma=False
    )
```
